32 devices in a mesh: dom: 8 (over z, y), feat: 4 (over x, core).
Axes of the slice: x: 2, y: 2, z: 4, core: 2. Of those that a mesh axis runs over, the one named last changes fastest.
Arguments:
- features: bfloat16 [32768, 512], P('dom', 'feat'), may hold values from -6 to 6
- theta: bfloat16 [512, 512], P(None, 'feat'), may hold values from -0.25 to 0.25
- incidence: int32 [3, 4096], P(None, 'dom'), may hold values from 0 to 4095, as said below
- edge_weight: float32 [16384], P('dom'), may hold values from 0.5 to 2
- cotangent: bfloat16 [32768, 512], P('dom', 'feat'), may hold values from -6 to 6
Outputs:
- activation: bfloat16 [32768, 512], P('dom', 'feat')
- grad_features: bfloat16 [32768, 512], P('dom', 'feat')
- grad_theta: float32 [512, 512], P('dom', 'feat')
The draws below stay inside these ranges and needn't reach their ends.
Inputs may be any that keep to these rules, and one draw needn't show every extreme that they name: `incidence`: in the 64 slots from one vertex owner to one hyperedge owner the live slots (weight over zero) come first, at least one of them; some hyperedge owner receives all 64 slots live from every vertex owner.
All inputs are finite; a program needn't handle non-finite values.
Results may differ from the reference program's by a relative error of at most 0.0073.
Values may be sent and summed in bfloat16 or wider, within the bound.
A program may use at most 64 MiB of HBM per device.

```python
import math
import jax
import jax.numpy as jnp
from jax import lax

F = 512
VTX_DEV = 4096
EDGE_DEV = 2048
CAP = 64
SLOTS = 512
VERTS = 32768
EDGES = 16384


def draw_incidence(key, part):
    owners = SLOTS // CAP
    key_order = jax.random.fold_in(key, 11)
    key_count = jax.random.fold_in(key, 12)
    key_weight = jax.random.fold_in(key, 13)
    key_vert = jax.random.fold_in(key, 14)
    key_edge = jax.random.fold_in(key, 15)
    order = jax.random.permutation(key_order, owners)
    hot = order < max(1, owners // 8)
    count = jax.random.randint(key_count, (owners, owners), 1, CAP // 2 + 1)
    count = jnp.where(hot[None, :], CAP, count)
    position = jnp.arange(CAP, dtype=jnp.int32)
    live = position[None, None, :] < count[:, :, None]
    weight = jnp.where(live, jax.random.randint(key_weight, (owners, owners, CAP), 1, 4), 0)
    vert = jax.random.randint(key_vert, (owners, owners, CAP), 0, VTX_DEV)
    edge = jax.random.randint(key_edge, (owners, owners, CAP), 0, EDGE_DEV)
    return jnp.stack([vert, edge, weight]).reshape(3, -1).astype(jnp.int32)


def raised(drawn, key, source, target, parts, factor):
    def block_of(dim):
        return (jnp.arange(drawn.shape[dim]) // (drawn.shape[dim] // parts)).reshape((-1,) + (1,) * (drawn.ndim - 1 - dim))

    first = jax.random.permutation(key, parts)[block_of(target)]
    second = (block_of(target) + parts // 2) % parts
    return jnp.where((block_of(source) == first) | (block_of(source) == second), factor * drawn, drawn)


def block_levels(own_key, shape, pieces, low, top_value):
    def one(dim, parts):
        heights = jax.random.uniform(jax.random.fold_in(jax.random.fold_in(own_key, 6), dim), (parts,), jnp.float32, low / len(pieces), top_value / len(pieces))
        return jnp.repeat(jnp.exp(heights), shape[dim] // parts).reshape((-1,) + (1,) * (len(shape) - dim - 1))

    level = one(*pieces[0])
    for cut in pieces[1:]:
        level = level * one(*cut)
    return level


def centred(rng, dims, scale, reach, cuts=(), kind=jnp.bfloat16):
    level = block_levels(rng, dims, cuts, -0.22, 0.18) if cuts else 1.0
    entries = jax.random.normal(rng, dims, jnp.float32) * scale * level
    return jnp.minimum(jnp.maximum(entries, -reach), reach).astype(kind)


def noise_with(rng, dims, deviation, bound, cuts, heavy, held_as=jnp.bfloat16):
    result = deviation * jax.random.normal(rng, dims, jnp.float32)
    if cuts:
        result = result * block_levels(rng, dims, cuts, -0.22, 0.18)
    return jnp.clip(raised(result, jax.random.fold_in(rng, 3), *heavy), -bound, bound).astype(held_as)


def setup_inputs(seed: int = 0) -> dict:
    key_of = jax.random.split(jax.random.key(seed), 6)
    features = noise_with(key_of[0], (VERTS, F), 1.0, 6.0, ((0, 8), (1, 4)), (0, 1, 8, 2.0))
    theta = centred(key_of[1], (F, F), F ** -0.5, 0.25, ((1, 4),))
    incidence = draw_incidence(jax.random.fold_in(key_of[5], 71), 0)
    edge_weight = jnp.clip(jnp.exp(math.log(2.0) - 1.3862944 * jax.random.uniform(key_of[3], (EDGES,), jnp.float32) ** block_levels(key_of[3], (EDGES,), ((0, 8),), -0.2, 0.2)), 0.5, 2.0)
    cotangent = centred(key_of[4], (VERTS, F), 1.0, 6.0, ((0, 8), (1, 4)))
    return {"features": features, "theta": theta, "incidence": incidence, "edge_weight": edge_weight, "cotangent": cotangent}


def slot_indices(incidence):
    total = incidence.shape[1]
    slot = jnp.arange(total, dtype=jnp.int32)
    source = slot // SLOTS
    target = slot % SLOTS // CAP
    vert = source * VTX_DEV + incidence[0].astype(jnp.int32)
    edge = target * EDGE_DEV + incidence[1].astype(jnp.int32)
    return (vert, edge)

def propagate(rows, vert, edge, weight, slot_scale, dvis, edge_scale):
    message = (slot_scale[:, None] * rows[vert].astype(jnp.float32)).astype(jnp.bfloat16)
    edge_sum = jax.ops.segment_sum(message.astype(jnp.float32), edge, num_segments=EDGES)
    edge_rows = (edge_scale[:, None] * edge_sum).astype(jnp.bfloat16)
    back = weight[:, None] * edge_rows[edge].astype(jnp.float32)
    return dvis[:, None] * jax.ops.segment_sum(back, vert, num_segments=VERTS)

def reference(features, theta, incidence, edge_weight, cotangent):
    vert, edge = slot_indices(incidence)
    weight = incidence[2].astype(jnp.float32)
    dv = 1.0 + jax.ops.segment_sum(weight, vert, num_segments=VERTS)
    dvis = lax.rsqrt(dv)
    de = 1.0 + jax.ops.segment_sum(weight, edge, num_segments=EDGES)
    edge_scale = edge_weight / de
    slot_scale = weight * dvis[vert]
    projected = jnp.dot(features, theta, preferred_element_type=jnp.float32).astype(jnp.bfloat16)
    width = min(F, 128)
    act_blocks = []
    grad_blocks = []
    for block in range(F // width):
        cols = slice(block * width, (block + 1) * width)
        summed = propagate(projected[:, cols], vert, edge, weight, slot_scale, dvis, edge_scale)
        sigma = jax.nn.sigmoid(summed)
        act_blocks.append((summed * sigma).astype(jnp.bfloat16))
        slope = sigma * (1.0 + summed * (1.0 - sigma))
        grad_summed = cotangent[:, cols].astype(jnp.float32) * slope
        grad_proj = propagate(grad_summed, vert, edge, weight, slot_scale, dvis, edge_scale)
        grad_blocks.append(grad_proj.astype(jnp.bfloat16))
    activation = jnp.concatenate(act_blocks, axis=1)
    grad_projected = jnp.concatenate(grad_blocks, axis=1)
    grad_features = jnp.dot(grad_projected, theta.T, preferred_element_type=jnp.float32).astype(jnp.bfloat16)
    grad_theta = jnp.dot(features.T, grad_projected, preferred_element_type=jnp.float32)
    return (activation, grad_features, grad_theta)
```

```python
import functools

import jax
import jax.numpy as jnp
from jax import lax
from jax.experimental import pallas as pl
from jax.experimental.pallas import tpu as pltpu
from jax.sharding import PartitionSpec as P

MESH = pl.DeviceIdType.MESH
LANES = 128
VMEM_BYTES = 40 * 1024 * 1024


def hi_lo_dot(mask, rows):
    hi = rows.astype(jnp.bfloat16)
    lo = (rows - hi.astype(jnp.float32)).astype(jnp.bfloat16)
    both = jnp.concatenate([hi, lo], axis=1)
    out = jnp.dot(mask, both, preferred_element_type=jnp.float32)
    half = rows.shape[1]
    return out[:, :half] + out[:, half:]


def layer_kernel(
    feat_ref, theta_ref, inc_ref, ew_ref, cot_ref,
    act_ref, gf_ref, gt_ref, rep_ref,
    meta, meta_send, meta_recv, meta_edge, v_mask, e_mask,
    x_send, x_recv, b_send, b_recv, gx_send, gx_recv, gb_send, gb_recv,
    theta_t, ax, gp, term, term_recv,
    dom_send, dom_recv, feat_send, feat_recv,
):
    owners, cap, cols = x_send.shape
    feats, slots, _ = ax.shape
    nvert = feat_ref.shape[0]
    share = gt_ref.shape[0]
    d = lax.axis_index("dom")
    f = lax.axis_index("feat")
    partner = f + 1 - 2 * lax.rem(f, 2)
    across = lax.rem(f + 2, 4)
    diagonal = lax.rem(partner + 2, 4)

    barrier = pltpu.get_barrier_semaphore()
    for k in range(1, owners):
        pl.semaphore_signal(
            barrier, inc=1, device_id=(lax.rem(d + k, owners), f), device_id_type=MESH
        )
    for other in (partner, across, diagonal):
        pl.semaphore_signal(barrier, inc=1, device_id=(d, other), device_id_type=MESH)

    pending = []

    def to_owners(phase, src, dst):
        copies = []
        for k in range(1, owners):
            peer = lax.rem(d + k, owners)
            copy = pltpu.make_async_remote_copy(
                src_ref=src.at[peer],
                dst_ref=dst.at[d],
                send_sem=dom_send.at[phase, k - 1],
                recv_sem=dom_recv.at[phase, k - 1],
                device_id=(peer, f),
                device_id_type=MESH,
            )
            copy.start()
            copies.append(copy)
        pending.extend(copies)
        dst[d] = src[d]
        return copies

    def to_feat(slot, src, dst, other):
        copy = pltpu.make_async_remote_copy(
            src_ref=src,
            dst_ref=dst,
            send_sem=feat_send.at[slot],
            recv_sem=feat_recv.at[slot],
            device_id=(d, other),
            device_id_type=MESH,
        )
        copy.start()
        pending.append(copy)
        return copy

    def arrived(copies):
        for copy in copies:
            copy.wait_recv()

    inc = inc_ref[...]
    vrow = inc[0:1, :]
    meta[...] = jnp.zeros_like(meta)
    meta[0:1, :] = vrow.astype(jnp.float32)
    meta[1:2, :] = inc[1:2, :].astype(jnp.float32)
    meta[2:3, :] = inc[2:3, :].astype(jnp.float32)
    wrow = meta[2:3, :]
    columns = jnp.transpose(meta[...])
    vcol = columns[:, 0:1].astype(jnp.int32)
    wcol = columns[:, 2:3]
    same = vcol == vrow
    v_mask[...] = jnp.where(same, 1.0, 0.0).astype(jnp.bfloat16)
    dvis_row = lax.rsqrt(1.0 + jnp.sum(jnp.where(same, wcol, 0.0), axis=0, keepdims=True))
    meta[3:4, :] = wrow * dvis_row

    mine = lax.rem(d, 2)
    for o in range(owners):
        tile = meta[:, o // 2 * LANES : (o // 2 + 1) * LANES]
        moved = pltpu.roll(tile, cap, 1)
        meta_send[o] = jnp.where(mine == o % 2, tile, moved)

    pl.semaphore_wait(barrier, owners - 1 + feats - 1)
    meta_copies = to_owners(0, meta_send, meta_recv)

    picked = jnp.zeros((slots, 2 * cols), jnp.float32)
    step = 512
    lane = lax.broadcasted_iota(jnp.int32, (slots, step), 1)
    for base in range(0, nvert, step):
        hit = jnp.where(vcol - base == lane, 1.0, 0.0).astype(jnp.bfloat16)
        both = jnp.concatenate(
            [feat_ref[base : base + step, :], cot_ref[base : base + step, :]], axis=1
        )
        picked = picked + jnp.dot(hit, both, preferred_element_type=jnp.float32)
    x_send[...] = picked[:, :cols].astype(jnp.bfloat16).reshape(owners, cap, cols)
    x_copies = to_owners(1, x_send, x_recv)
    cot = picked[:, cols:]

    theta_copies = []
    for slot, other in enumerate((partner, across, diagonal)):
        theta_copies.append(
            to_feat(
                slot,
                theta_ref.at[pl.ds(pl.multiple_of(other * cols, cols), cols), :],
                theta_t.at[f],
                other,
            )
        )
    theta_t[f] = theta_ref[pl.ds(pl.multiple_of(f * cols, cols), cols), :]

    dvis = lax.rsqrt(1.0 + jnp.sum(jnp.where(same, wrow, 0.0), axis=1, keepdims=True))
    scale = wcol * dvis
    sub_i = lax.broadcasted_iota(jnp.int32, (slots, slots), 0)
    lane_i = lax.broadcasted_iota(jnp.int32, (slots, slots), 1)
    later_row = jnp.sum(
        jnp.where(same, jnp.where(sub_i < lane_i, 1.0, 0.0), 0.0), axis=0, keepdims=True
    )
    later_col = jnp.sum(
        jnp.where(same, jnp.where(lane_i < sub_i, 1.0, 0.0), 0.0), axis=1, keepdims=True
    )
    rep_ref[...] = jnp.where(later_row > 0.0, -1, vrow)

    arrived(meta_copies)
    half = lax.broadcasted_iota(jnp.int32, (8, LANES), 1) < cap
    for q in range(owners // 2):
        meta_edge[:, q * LANES : (q + 1) * LANES] = jnp.where(
            half, meta_recv[2 * q], meta_recv[2 * q + 1]
        )
    ecolumns = jnp.transpose(meta_edge[...])
    ecol = ecolumns[:, 1:2]
    same_edge = ecol == meta_edge[1:2, :]
    e_mask[...] = jnp.where(same_edge, 1.0, 0.0).astype(jnp.bfloat16)
    degree = 1.0 + jnp.sum(
        jnp.where(same_edge, meta_edge[2:3, :], 0.0), axis=1, keepdims=True
    )
    sent_scale = ecolumns[:, 3:4]
    eint = ecol.astype(jnp.int32)
    groups = ew_ref.shape[0]
    eweight = jnp.zeros((slots, LANES), jnp.float32)
    for g in range(groups):
        near = lax.broadcasted_iota(jnp.int32, (slots, LANES), 1) + g * LANES
        eweight = jnp.where(eint == near, ew_ref[g : g + 1, :], eweight)
    edge_scale = jnp.sum(eweight, axis=1, keepdims=True) / degree

    arrived(x_copies)
    rows = x_recv[...].reshape(slots, cols).astype(jnp.float32) * sent_scale
    b_send[...] = (
        (edge_scale * hi_lo_dot(e_mask[...], rows))
        .astype(jnp.bfloat16)
        .reshape(owners, cap, cols)
    )
    b_copies = to_owners(2, b_send, b_recv)

    def gather_feat(slot, buf, use):
        near = to_feat(slot, buf.at[f], buf.at[f], partner)
        far = to_feat(slot + 1, buf.at[f], buf.at[f], across)
        total = use(f)
        near.wait_recv()
        total = total + use(partner)
        far.wait_recv()
        relay = to_feat(slot + 2, buf.at[across], buf.at[across], partner)
        total = total + use(across)
        relay.wait_recv()
        return total + use(diagonal)

    arrived(b_copies)
    back = wcol * b_recv[...].reshape(slots, cols).astype(jnp.float32)
    ax[f] = (dvis * hi_lo_dot(v_mask[...], back)).astype(jnp.bfloat16)
    summed = gather_feat(
        3,
        ax,
        lambda j: jnp.dot(
            ax[j],
            theta_ref[pl.ds(pl.multiple_of(j * cols, cols), cols), :],
            preferred_element_type=jnp.float32,
        ),
    )
    sigma = jax.nn.sigmoid(summed)
    grad = cot * (sigma * (1.0 + summed * (1.0 - sigma)))
    gx_send[...] = (scale * grad).astype(jnp.bfloat16).reshape(owners, cap, cols)
    gx_copies = to_owners(3, gx_send, gx_recv)
    act_ref[...] = (summed * sigma).astype(jnp.bfloat16)

    once = jnp.where(later_col > 0.0, 0.0, grad).astype(jnp.bfloat16)
    per = cols // share
    for j in range(feats):
        part = lax.dot_general(
            ax[j], once, (((0,), (0,)), ((), ())), preferred_element_type=jnp.float32
        )
        term[j * per : (j + 1) * per] = part.reshape(per, share, cols)

    arrived(gx_copies)
    esum = jnp.dot(
        e_mask[...], gx_recv[...].reshape(slots, cols), preferred_element_type=jnp.float32
    )
    gb_send[...] = (edge_scale * esum).astype(jnp.bfloat16).reshape(owners, cap, cols)
    gb_copies = to_owners(4, gb_send, gb_recv)
    term_copies = to_owners(5, term, term_recv)

    arrived(gb_copies)
    gback = wcol * gb_recv[...].reshape(slots, cols).astype(jnp.float32)
    gp[f] = (dvis * hi_lo_dot(v_mask[...], gback)).astype(jnp.bfloat16)
    arrived(theta_copies)
    gfeat = gather_feat(
        6,
        gp,
        lambda j: lax.dot_general(
            gp[j], theta_t[j], (((1,), (1,)), ((), ())), preferred_element_type=jnp.float32
        ),
    )
    gf_ref[...] = gfeat.astype(jnp.bfloat16)
    arrived(term_copies)
    gt_ref[...] = jnp.sum(term_recv[...], axis=0)
    for copy in pending:
        copy.wait_send()


def spread_kernel(rep_ref, act_ref, gf_ref, act_out, gf_out):
    rows, cols = act_out.shape
    slots = act_ref.shape[0]
    base = pl.program_id(0) * rows
    vertex = lax.broadcasted_iota(jnp.int32, (rows, slots), 0) + base
    hit = jnp.where(vertex == rep_ref[...], 1.0, 0.0).astype(jnp.bfloat16)
    both = jnp.concatenate([act_ref[...], gf_ref[...]], axis=1)
    out = jnp.dot(hit, both, preferred_element_type=jnp.float32)
    act_out[...] = out[:, :cols].astype(act_out.dtype)
    gf_out[...] = out[:, cols:].astype(gf_out.dtype)


def compact(features, theta, incidence, edge_weight, cotangent):
    owners = lax.axis_size("dom")
    feats = lax.axis_size("feat")
    nvert, cols = features.shape
    slots = incidence.shape[1]
    cap = slots // owners
    share = theta.shape[0] // owners
    bf16, f32 = jnp.bfloat16, jnp.float32
    vmem = pl.BlockSpec(memory_space=pltpu.VMEM)
    block = pltpu.VMEM((owners, cap, cols), bf16)
    act, gf, gt, rep = pl.pallas_call(
        layer_kernel,
        out_shape=(
            jax.ShapeDtypeStruct((slots, cols), bf16),
            jax.ShapeDtypeStruct((slots, cols), bf16),
            jax.ShapeDtypeStruct((share, cols), f32),
            jax.ShapeDtypeStruct((1, slots), jnp.int32),
        ),
        in_specs=[vmem] * 5,
        out_specs=(vmem,) * 4,
        scratch_shapes=[
            pltpu.VMEM((8, slots), f32),
            pltpu.VMEM((owners, 8, LANES), f32),
            pltpu.VMEM((owners, 8, LANES), f32),
            pltpu.VMEM((8, slots), f32),
            pltpu.VMEM((slots, slots), bf16),
            pltpu.VMEM((slots, slots), bf16),
        ]
        + [block] * 8
        + [
            pltpu.VMEM((feats, cols, cols), bf16),
            pltpu.VMEM((feats, slots, cols), bf16),
            pltpu.VMEM((feats, slots, cols), bf16),
            pltpu.VMEM((owners, share, cols), f32),
            pltpu.VMEM((owners, share, cols), f32),
            pltpu.SemaphoreType.DMA((6, owners - 1)),
            pltpu.SemaphoreType.DMA((6, owners - 1)),
            pltpu.SemaphoreType.DMA((9,)),
            pltpu.SemaphoreType.DMA((9,)),
        ],
        compiler_params=pltpu.CompilerParams(
            collective_id=0, has_side_effects=True, vmem_limit_bytes=VMEM_BYTES
        ),
        name="layer",
    )(features, theta, incidence, edge_weight.reshape(-1, LANES), cotangent)
    rows = 1024
    whole = lambda i: (0, 0)
    activation, grad_features = pl.pallas_call(
        spread_kernel,
        grid=(nvert // rows,),
        out_shape=(jax.ShapeDtypeStruct((nvert, cols), bf16),) * 2,
        in_specs=[
            pl.BlockSpec((1, slots), whole),
            pl.BlockSpec((slots, cols), whole),
            pl.BlockSpec((slots, cols), whole),
        ],
        out_specs=(pl.BlockSpec((rows, cols), lambda i: (i, 0)),) * 2,
        compiler_params=pltpu.CompilerParams(vmem_limit_bytes=VMEM_BYTES),
        name="spread",
    )(rep, act, gf)
    return activation, grad_features, gt


def local(features, theta, incidence, edge_weight, cotangent):
    owners = lax.axis_size("dom")
    nvert = features.shape[0]
    cols = features.shape[1]
    nedge = edge_weight.shape[0]
    vert = incidence[0]
    edge = incidence[1]
    weight = incidence[2]
    weight_f = weight.astype(jnp.float32)
    dvis = lax.rsqrt(1.0 + jax.ops.segment_sum(weight_f, vert, num_segments=nvert))
    slot_scale = weight_f * dvis[vert]
    full_rows = lax.all_gather(features, "feat", axis=1, tiled=True)
    projected = jnp.dot(full_rows, theta, preferred_element_type=jnp.float32).astype(jnp.bfloat16)
    message = (slot_scale[:, None] * projected[vert].astype(jnp.float32)).astype(jnp.bfloat16)
    recv_rows, recv_edge, recv_weight = (
        lax.all_to_all(
            message.reshape(owners, -1, cols), "dom", split_axis=0, concat_axis=0, tiled=True
        ),
        lax.all_to_all(edge.reshape(owners, -1), "dom", split_axis=0, concat_axis=0, tiled=True),
        lax.all_to_all(weight.reshape(owners, -1), "dom", split_axis=0, concat_axis=0, tiled=True),
    )
    recv_edge = recv_edge.reshape(-1)
    degree = 1.0 + jax.ops.segment_sum(
        recv_weight.reshape(-1).astype(jnp.float32), recv_edge, num_segments=nedge
    )
    edge_scale = edge_weight / degree

    def edge_side(rows):
        edge_sum = jax.ops.segment_sum(
            rows.reshape(-1, cols).astype(jnp.float32), recv_edge, num_segments=nedge
        )
        edge_rows = (edge_scale[:, None] * edge_sum).astype(jnp.bfloat16)
        return edge_rows[recv_edge].reshape(owners, -1, cols)

    def vertex_side(back):
        terms = weight_f[:, None] * back.reshape(-1, cols).astype(jnp.float32)
        return dvis[:, None] * jax.ops.segment_sum(terms, vert, num_segments=nvert)

    back = lax.all_to_all(edge_side(recv_rows), "dom", split_axis=0, concat_axis=0, tiled=True)
    summed = vertex_side(back)
    sigma = jax.nn.sigmoid(summed)
    activation = (summed * sigma).astype(jnp.bfloat16)
    slope = sigma * (1.0 + summed * (1.0 - sigma))
    grad_summed = cotangent.astype(jnp.float32) * slope
    grad_message = (slot_scale[:, None] * grad_summed[vert]).astype(jnp.bfloat16)
    grad_recv = lax.all_to_all(
        grad_message.reshape(owners, -1, cols), "dom", split_axis=0, concat_axis=0, tiled=True
    )
    grad_back = lax.all_to_all(edge_side(grad_recv), "dom", split_axis=0, concat_axis=0, tiled=True)
    grad_projected = vertex_side(grad_back).astype(jnp.bfloat16)
    theta_full = lax.all_gather(theta, "feat", axis=1, tiled=True)
    theta_mine = lax.dynamic_slice_in_dim(theta_full, lax.axis_index("feat") * cols, cols, 0)
    grad_total = lax.dot_general(
        lax.all_gather(grad_projected, "feat", axis=1, tiled=True),
        theta_mine,
        (((1,), (1,)), ((), ())),
        preferred_element_type=jnp.float32,
    )
    grad_features = grad_total.astype(jnp.bfloat16)
    share = full_rows.shape[1] // owners
    term = lax.dot_general(
        full_rows, grad_projected, (((0,), (0,)), ((), ())), preferred_element_type=jnp.float32
    )
    total = lax.psum(term, "dom")
    grad_theta = lax.dynamic_slice_in_dim(total, lax.axis_index("dom") * share, share, 0)
    return (activation, grad_features, grad_theta)


def solution(mesh):
    placed = (P("dom", "feat"), P(None, "feat"), P(None, "dom"), P("dom"), P("dom", "feat"))
    owners, feats = mesh.shape["dom"], mesh.shape["feat"]

    def program(features, theta, incidence, edge_weight, cotangent):
        nvert, cols = features.shape
        slots, nedge = incidence.shape[1], edge_weight.shape[0]
        fits = (
            feats == 4
            and cols == LANES
            and owners % 2 == 0
            and slots == owners * LANES // 2
            and slots <= 1024
            and nvert % 1024 == 0
            and nedge % LANES == 0
            and theta.shape[0] % (16 * owners) == 0
            and cols % (theta.shape[0] // owners) == 0
        )
        run = compact if fits else local
        return run(features, theta, incidence, edge_weight, cotangent)

    return jax.shard_map(
        program,
        mesh=mesh,
        in_specs=placed,
        out_specs=(P("dom", "feat"), P("dom", "feat"), P("dom", "feat")),
        check_vma=False,
    )
```

```python
import functools

import jax
import jax.numpy as jnp
from jax import lax
from jax.experimental import pallas as pl
from jax.experimental.pallas import tpu as pltpu
from jax.sharding import PartitionSpec as P

MESH = pl.DeviceIdType.MESH
LANES = 128
VMEM_BYTES = 62 * 1024 * 1024


def hi_lo_dot(mask, rows):
    hi = rows.astype(jnp.bfloat16)
    lo = (rows - hi.astype(jnp.float32)).astype(jnp.bfloat16)
    both = jnp.concatenate([hi, lo], axis=1)
    out = jnp.dot(mask, both, preferred_element_type=jnp.float32)
    half = rows.shape[1]
    return out[:, :half] + out[:, half:]


def layer_kernel(
    feat_hbm, theta_hbm, inc_hbm, ew_hbm, cot_hbm,
    act_ref, gf_ref, gt_ref, rep_ref,
    feat_ref, theta_ref, inc_ref, ew_ref, cot_ref, load_sem,
    meta, meta_send, meta_recv, meta_edge, v_mask, e_mask,
    x_send, x_recv, b_send, b_recv, gx_send, gx_recv, gb_send, gb_recv,
    theta_t, ax, gp, term, term_recv,
    dom_send, dom_recv, feat_send, feat_recv,
):
    owners, cap, cols = x_send.shape
    feats, slots, _ = ax.shape
    nvert = feat_ref.shape[0]
    share = gt_ref.shape[0]
    d = lax.axis_index("dom")
    f = lax.axis_index("feat")
    partner = f + 1 - 2 * lax.rem(f, 2)
    across = lax.rem(f + 2, 4)
    diagonal = lax.rem(partner + 2, 4)

    loads = []
    for n, (src, dst) in enumerate(
        (
            (inc_hbm, inc_ref),
            (feat_hbm, feat_ref),
            (cot_hbm, cot_ref),
            (theta_hbm, theta_ref),
            (ew_hbm, ew_ref),
        )
    ):
        load = pltpu.make_async_copy(src, dst, load_sem.at[n])
        load.start()
        loads.append(load)

    barrier = pltpu.get_barrier_semaphore()
    for k in range(1, owners):
        pl.semaphore_signal(
            barrier, inc=1, device_id=(lax.rem(d + k, owners), f), device_id_type=MESH
        )
    for other in (partner, across, diagonal):
        pl.semaphore_signal(barrier, inc=1, device_id=(d, other), device_id_type=MESH)

    pending = []

    def to_owners(phase, src, dst):
        copies = []
        for k in range(1, owners):
            peer = lax.rem(d + k, owners)
            copy = pltpu.make_async_remote_copy(
                src_ref=src.at[peer],
                dst_ref=dst.at[d],
                send_sem=dom_send.at[phase, k - 1],
                recv_sem=dom_recv.at[phase, k - 1],
                device_id=(peer, f),
                device_id_type=MESH,
            )
            copy.start()
            copies.append(copy)
        pending.extend(copies)
        dst[d] = src[d]
        return copies

    def to_feat(slot, src, dst, other):
        copy = pltpu.make_async_remote_copy(
            src_ref=src,
            dst_ref=dst,
            send_sem=feat_send.at[slot],
            recv_sem=feat_recv.at[slot],
            device_id=(d, other),
            device_id_type=MESH,
        )
        copy.start()
        pending.append(copy)
        return copy

    def arrived(copies):
        for copy in copies:
            copy.wait_recv()

    loads[0].wait()
    inc = inc_ref[...]
    vrow = inc[0:1, :]
    meta[...] = jnp.zeros_like(meta)
    meta[0:1, :] = vrow.astype(jnp.float32)
    meta[1:2, :] = inc[1:2, :].astype(jnp.float32)
    meta[2:3, :] = inc[2:3, :].astype(jnp.float32)
    wrow = meta[2:3, :]
    columns = jnp.transpose(meta[...])
    vcol = columns[:, 0:1].astype(jnp.int32)
    wcol = columns[:, 2:3]
    same = vcol == vrow
    v_mask[...] = jnp.where(same, 1.0, 0.0).astype(jnp.bfloat16)
    dvis_row = lax.rsqrt(1.0 + jnp.sum(jnp.where(same, wcol, 0.0), axis=0, keepdims=True))
    meta[3:4, :] = wrow * dvis_row

    mine = lax.rem(d, 2)
    for o in range(owners):
        tile = meta[:, o // 2 * LANES : (o // 2 + 1) * LANES]
        moved = pltpu.roll(tile, cap, 1)
        meta_send[o] = jnp.where(mine == o % 2, tile, moved)

    loads[1].wait()
    loads[2].wait()
    picked = jnp.zeros((slots, 2 * cols), jnp.float32)
    step = 512
    lane = lax.broadcasted_iota(jnp.int32, (slots, step), 1)
    for base in range(0, nvert, step):
        hit = jnp.where(vcol - base == lane, 1.0, 0.0).astype(jnp.bfloat16)
        both = jnp.concatenate(
            [feat_ref[base : base + step, :], cot_ref[base : base + step, :]], axis=1
        )
        picked = picked + jnp.dot(hit, both, preferred_element_type=jnp.float32)
    x_send[...] = picked[:, :cols].astype(jnp.bfloat16).reshape(owners, cap, cols)
    pl.semaphore_wait(barrier, owners - 1 + feats - 1)
    meta_copies = to_owners(0, meta_send, meta_recv)
    x_copies = to_owners(1, x_send, x_recv)
    cot = picked[:, cols:]

    loads[3].wait()
    theta_copies = []
    for slot, other in enumerate((partner, across, diagonal)):
        theta_copies.append(
            to_feat(
                slot,
                theta_ref.at[pl.ds(pl.multiple_of(other * cols, cols), cols), :],
                theta_t.at[f],
                other,
            )
        )
    theta_t[f] = theta_ref[pl.ds(pl.multiple_of(f * cols, cols), cols), :]

    dvis = lax.rsqrt(1.0 + jnp.sum(jnp.where(same, wrow, 0.0), axis=1, keepdims=True))
    scale = wcol * dvis
    sub_i = lax.broadcasted_iota(jnp.int32, (slots, slots), 0)
    lane_i = lax.broadcasted_iota(jnp.int32, (slots, slots), 1)
    later_row = jnp.sum(
        jnp.where(same, jnp.where(sub_i < lane_i, 1.0, 0.0), 0.0), axis=0, keepdims=True
    )
    later_col = jnp.sum(
        jnp.where(same, jnp.where(lane_i < sub_i, 1.0, 0.0), 0.0), axis=1, keepdims=True
    )
    rep_ref[...] = jnp.where(later_row > 0.0, -1, vrow)

    arrived(meta_copies)
    half = lax.broadcasted_iota(jnp.int32, (8, LANES), 1) < cap
    for q in range(owners // 2):
        meta_edge[:, q * LANES : (q + 1) * LANES] = jnp.where(
            half, meta_recv[2 * q], meta_recv[2 * q + 1]
        )
    ecolumns = jnp.transpose(meta_edge[...])
    ecol = ecolumns[:, 1:2]
    same_edge = ecol == meta_edge[1:2, :]
    e_mask[...] = jnp.where(same_edge, 1.0, 0.0).astype(jnp.bfloat16)
    degree = 1.0 + jnp.sum(
        jnp.where(same_edge, meta_edge[2:3, :], 0.0), axis=1, keepdims=True
    )
    sent_scale = ecolumns[:, 3:4]
    eint = ecol.astype(jnp.int32)
    loads[4].wait()
    groups = ew_ref.shape[0]
    eweight = jnp.zeros((slots, LANES), jnp.float32)
    for g in range(groups):
        near = lax.broadcasted_iota(jnp.int32, (slots, LANES), 1) + g * LANES
        eweight = jnp.where(eint == near, ew_ref[g : g + 1, :], eweight)
    edge_scale = jnp.sum(eweight, axis=1, keepdims=True) / degree

    arrived(x_copies)
    rows = x_recv[...].reshape(slots, cols).astype(jnp.float32) * sent_scale
    b_send[...] = (
        (edge_scale * hi_lo_dot(e_mask[...], rows))
        .astype(jnp.bfloat16)
        .reshape(owners, cap, cols)
    )
    b_copies = to_owners(2, b_send, b_recv)

    def gather_feat(slot, buf, use):
        near = to_feat(slot, buf.at[f], buf.at[f], partner)
        far = to_feat(slot + 1, buf.at[f], buf.at[f], across)
        total = use(f)
        near.wait_recv()
        total = total + use(partner)
        far.wait_recv()
        relay = to_feat(slot + 2, buf.at[across], buf.at[across], partner)
        total = total + use(across)
        relay.wait_recv()
        return total + use(diagonal)

    arrived(b_copies)
    back = wcol * b_recv[...].reshape(slots, cols).astype(jnp.float32)
    ax[f] = (dvis * hi_lo_dot(v_mask[...], back)).astype(jnp.bfloat16)
    summed = gather_feat(
        3,
        ax,
        lambda j: jnp.dot(
            ax[j],
            theta_ref[pl.ds(pl.multiple_of(j * cols, cols), cols), :],
            preferred_element_type=jnp.float32,
        ),
    )
    sigma = jax.nn.sigmoid(summed)
    grad = cot * (sigma * (1.0 + summed * (1.0 - sigma)))
    gx_send[...] = (scale * grad).astype(jnp.bfloat16).reshape(owners, cap, cols)
    gx_copies = to_owners(3, gx_send, gx_recv)
    act_ref[...] = (summed * sigma).astype(jnp.bfloat16)

    once = jnp.where(later_col > 0.0, 0.0, grad).astype(jnp.bfloat16)
    per = cols // share
    for j in range(feats):
        part = lax.dot_general(
            ax[j], once, (((0,), (0,)), ((), ())), preferred_element_type=jnp.float32
        )
        term[j * per : (j + 1) * per] = part.reshape(per, share, cols)

    arrived(gx_copies)
    esum = jnp.dot(
        e_mask[...], gx_recv[...].reshape(slots, cols), preferred_element_type=jnp.float32
    )
    gb_send[...] = (edge_scale * esum).astype(jnp.bfloat16).reshape(owners, cap, cols)
    gb_copies = to_owners(4, gb_send, gb_recv)
    term_copies = to_owners(5, term, term_recv)

    arrived(gb_copies)
    gback = wcol * gb_recv[...].reshape(slots, cols).astype(jnp.float32)
    gp[f] = (dvis * hi_lo_dot(v_mask[...], gback)).astype(jnp.bfloat16)
    arrived(theta_copies)
    gfeat = gather_feat(
        6,
        gp,
        lambda j: lax.dot_general(
            gp[j], theta_t[j], (((1,), (1,)), ((), ())), preferred_element_type=jnp.float32
        ),
    )
    gf_ref[...] = gfeat.astype(jnp.bfloat16)
    arrived(term_copies)
    gt_ref[...] = jnp.sum(term_recv[...], axis=0)
    for copy in pending:
        copy.wait_send()


def spread_kernel(rep_ref, act_ref, gf_ref, act_out, gf_out):
    rows, cols = act_out.shape
    slots = act_ref.shape[0]
    base = pl.program_id(0) * rows
    vertex = lax.broadcasted_iota(jnp.int32, (rows, slots), 0) + base
    hit = jnp.where(vertex == rep_ref[...], 1.0, 0.0).astype(jnp.bfloat16)
    both = jnp.concatenate([act_ref[...], gf_ref[...]], axis=1)
    out = jnp.dot(hit, both, preferred_element_type=jnp.float32)
    act_out[...] = out[:, :cols].astype(act_out.dtype)
    gf_out[...] = out[:, cols:].astype(gf_out.dtype)


def compact(features, theta, incidence, edge_weight, cotangent):
    owners = lax.axis_size("dom")
    feats = lax.axis_size("feat")
    nvert, cols = features.shape
    slots = incidence.shape[1]
    cap = slots // owners
    share = theta.shape[0] // owners
    bf16, f32 = jnp.bfloat16, jnp.float32
    vmem = pl.BlockSpec(memory_space=pltpu.VMEM)
    block = pltpu.VMEM((owners, cap, cols), bf16)
    act, gf, gt, rep = pl.pallas_call(
        layer_kernel,
        out_shape=(
            jax.ShapeDtypeStruct((slots, cols), bf16),
            jax.ShapeDtypeStruct((slots, cols), bf16),
            jax.ShapeDtypeStruct((share, cols), f32),
            jax.ShapeDtypeStruct((1, slots), jnp.int32),
        ),
        in_specs=[pl.BlockSpec(memory_space=pltpu.HBM)] * 5,
        out_specs=(vmem,) * 4,
        scratch_shapes=[
            pltpu.VMEM(features.shape, bf16),
            pltpu.VMEM(theta.shape, bf16),
            pltpu.VMEM(incidence.shape, jnp.int32),
            pltpu.VMEM((edge_weight.shape[0] // LANES, LANES), f32),
            pltpu.VMEM(cotangent.shape, bf16),
            pltpu.SemaphoreType.DMA((5,)),
            pltpu.VMEM((8, slots), f32),
            pltpu.VMEM((owners, 8, LANES), f32),
            pltpu.VMEM((owners, 8, LANES), f32),
            pltpu.VMEM((8, slots), f32),
            pltpu.VMEM((slots, slots), bf16),
            pltpu.VMEM((slots, slots), bf16),
        ]
        + [block] * 8
        + [
            pltpu.VMEM((feats, cols, cols), bf16),
            pltpu.VMEM((feats, slots, cols), bf16),
            pltpu.VMEM((feats, slots, cols), bf16),
            pltpu.VMEM((owners, share, cols), f32),
            pltpu.VMEM((owners, share, cols), f32),
            pltpu.SemaphoreType.DMA((6, owners - 1)),
            pltpu.SemaphoreType.DMA((6, owners - 1)),
            pltpu.SemaphoreType.DMA((9,)),
            pltpu.SemaphoreType.DMA((9,)),
        ],
        compiler_params=pltpu.CompilerParams(
            collective_id=0, has_side_effects=True, vmem_limit_bytes=VMEM_BYTES
        ),
        name="layer",
    )(features, theta, incidence, edge_weight.reshape(-1, LANES), cotangent)
    rows = 1024
    whole = lambda i: (0, 0)
    activation, grad_features = pl.pallas_call(
        spread_kernel,
        grid=(nvert // rows,),
        out_shape=(jax.ShapeDtypeStruct((nvert, cols), bf16),) * 2,
        in_specs=[
            pl.BlockSpec((1, slots), whole),
            pl.BlockSpec((slots, cols), whole),
            pl.BlockSpec((slots, cols), whole),
        ],
        out_specs=(pl.BlockSpec((rows, cols), lambda i: (i, 0)),) * 2,
        compiler_params=pltpu.CompilerParams(vmem_limit_bytes=VMEM_BYTES),
        name="spread",
    )(rep, act, gf)
    return activation, grad_features, gt


def local(features, theta, incidence, edge_weight, cotangent):
    owners = lax.axis_size("dom")
    nvert = features.shape[0]
    cols = features.shape[1]
    nedge = edge_weight.shape[0]
    vert = incidence[0]
    edge = incidence[1]
    weight = incidence[2]
    weight_f = weight.astype(jnp.float32)
    dvis = lax.rsqrt(1.0 + jax.ops.segment_sum(weight_f, vert, num_segments=nvert))
    slot_scale = weight_f * dvis[vert]
    full_rows = lax.all_gather(features, "feat", axis=1, tiled=True)
    projected = jnp.dot(full_rows, theta, preferred_element_type=jnp.float32).astype(jnp.bfloat16)
    message = (slot_scale[:, None] * projected[vert].astype(jnp.float32)).astype(jnp.bfloat16)
    recv_rows, recv_edge, recv_weight = (
        lax.all_to_all(
            message.reshape(owners, -1, cols), "dom", split_axis=0, concat_axis=0, tiled=True
        ),
        lax.all_to_all(edge.reshape(owners, -1), "dom", split_axis=0, concat_axis=0, tiled=True),
        lax.all_to_all(weight.reshape(owners, -1), "dom", split_axis=0, concat_axis=0, tiled=True),
    )
    recv_edge = recv_edge.reshape(-1)
    degree = 1.0 + jax.ops.segment_sum(
        recv_weight.reshape(-1).astype(jnp.float32), recv_edge, num_segments=nedge
    )
    edge_scale = edge_weight / degree

    def edge_side(rows):
        edge_sum = jax.ops.segment_sum(
            rows.reshape(-1, cols).astype(jnp.float32), recv_edge, num_segments=nedge
        )
        edge_rows = (edge_scale[:, None] * edge_sum).astype(jnp.bfloat16)
        return edge_rows[recv_edge].reshape(owners, -1, cols)

    def vertex_side(back):
        terms = weight_f[:, None] * back.reshape(-1, cols).astype(jnp.float32)
        return dvis[:, None] * jax.ops.segment_sum(terms, vert, num_segments=nvert)

    back = lax.all_to_all(edge_side(recv_rows), "dom", split_axis=0, concat_axis=0, tiled=True)
    summed = vertex_side(back)
    sigma = jax.nn.sigmoid(summed)
    activation = (summed * sigma).astype(jnp.bfloat16)
    slope = sigma * (1.0 + summed * (1.0 - sigma))
    grad_summed = cotangent.astype(jnp.float32) * slope
    grad_message = (slot_scale[:, None] * grad_summed[vert]).astype(jnp.bfloat16)
    grad_recv = lax.all_to_all(
        grad_message.reshape(owners, -1, cols), "dom", split_axis=0, concat_axis=0, tiled=True
    )
    grad_back = lax.all_to_all(edge_side(grad_recv), "dom", split_axis=0, concat_axis=0, tiled=True)
    grad_projected = vertex_side(grad_back).astype(jnp.bfloat16)
    theta_full = lax.all_gather(theta, "feat", axis=1, tiled=True)
    theta_mine = lax.dynamic_slice_in_dim(theta_full, lax.axis_index("feat") * cols, cols, 0)
    grad_total = lax.dot_general(
        lax.all_gather(grad_projected, "feat", axis=1, tiled=True),
        theta_mine,
        (((1,), (1,)), ((), ())),
        preferred_element_type=jnp.float32,
    )
    grad_features = grad_total.astype(jnp.bfloat16)
    share = full_rows.shape[1] // owners
    term = lax.dot_general(
        full_rows, grad_projected, (((0,), (0,)), ((), ())), preferred_element_type=jnp.float32
    )
    total = lax.psum(term, "dom")
    grad_theta = lax.dynamic_slice_in_dim(total, lax.axis_index("dom") * share, share, 0)
    return (activation, grad_features, grad_theta)


def solution(mesh):
    placed = (P("dom", "feat"), P(None, "feat"), P(None, "dom"), P("dom"), P("dom", "feat"))
    owners, feats = mesh.shape["dom"], mesh.shape["feat"]

    def program(features, theta, incidence, edge_weight, cotangent):
        nvert, cols = features.shape
        slots, nedge = incidence.shape[1], edge_weight.shape[0]
        fits = (
            feats == 4
            and cols == LANES
            and owners % 2 == 0
            and slots == owners * LANES // 2
            and slots <= 1024
            and nvert % 1024 == 0
            and nedge % LANES == 0
            and theta.shape[0] % (16 * owners) == 0
            and cols % (theta.shape[0] // owners) == 0
        )
        run = compact if fits else local
        return run(features, theta, incidence, edge_weight, cotangent)

    return jax.shard_map(
        program,
        mesh=mesh,
        in_specs=placed,
        out_specs=(P("dom", "feat"), P("dom", "feat"), P("dom", "feat")),
        check_vma=False,
    )
```

```python
import functools

import jax
import jax.numpy as jnp
from jax import lax
from jax.experimental import pallas as pl
from jax.experimental.pallas import tpu as pltpu
from jax.sharding import PartitionSpec as P

MESH = pl.DeviceIdType.MESH
LANES = 128
VMEM_BYTES = 62 * 1024 * 1024


def hi_lo_dot(mask, rows):
    hi = rows.astype(jnp.bfloat16)
    lo = (rows - hi.astype(jnp.float32)).astype(jnp.bfloat16)
    both = jnp.concatenate([hi, lo], axis=1)
    out = jnp.dot(mask, both, preferred_element_type=jnp.float32)
    half = rows.shape[1]
    return out[:, :half] + out[:, half:]


def layer_kernel(
    feat_hbm, theta_hbm, inc_hbm, ew_hbm, cot_hbm,
    act_ref, gf_ref, gt_ref, rep_ref,
    feat_ref, theta_ref, inc_ref, ew_ref, cot_ref, load_sem,
    meta, meta_send, meta_recv, meta_edge, v_mask, e_mask,
    x_send, x_recv, b_send, b_recv, gx_send, gx_recv, gb_send, gb_recv,
    theta, cot, ax, grads, acts, term, term_recv,
    dom_send, dom_recv, feat_send, feat_recv,
):
    owners, cap, cols = x_send.shape
    slots = ax.shape[0]
    feats = ax.shape[1] // cols
    nvert = feat_ref.shape[0]
    share = gt_ref.shape[0]
    d = lax.axis_index("dom")
    f = lax.axis_index("feat")
    partner = f + 1 - 2 * lax.rem(f, 2)
    across = lax.rem(f + 2, 4)
    diagonal = lax.rem(partner + 2, 4)

    loads = []
    for n, (src, dst) in enumerate(
        (
            (inc_hbm, inc_ref),
            (feat_hbm, feat_ref),
            (cot_hbm, cot_ref),
            (theta_hbm, theta_ref),
            (ew_hbm, ew_ref),
        )
    ):
        load = pltpu.make_async_copy(src, dst, load_sem.at[n])
        load.start()
        loads.append(load)

    barrier = pltpu.get_barrier_semaphore()
    for k in range(1, owners):
        pl.semaphore_signal(
            barrier, inc=1, device_id=(lax.rem(d + k, owners), f), device_id_type=MESH
        )
    for other in (partner, across, diagonal):
        pl.semaphore_signal(barrier, inc=1, device_id=(d, other), device_id_type=MESH)

    pending = []

    def to_owners(phase, src, dst):
        copies = []
        for k in range(1, owners):
            peer = lax.rem(d + k, owners)
            copy = pltpu.make_async_remote_copy(
                src_ref=src.at[peer],
                dst_ref=dst.at[d],
                send_sem=dom_send.at[phase, k - 1],
                recv_sem=dom_recv.at[phase, k - 1],
                device_id=(peer, f),
                device_id_type=MESH,
            )
            copy.start()
            copies.append(copy)
        pending.extend(copies)
        dst[d] = src[d]
        return copies

    def to_feat(slot, p, src, dst, other):
        copy = pltpu.make_async_remote_copy(
            src_ref=src,
            dst_ref=dst,
            send_sem=feat_send.at[slot, p],
            recv_sem=feat_recv.at[slot, p],
            device_id=(d, other),
            device_id_type=MESH,
        )
        copy.start()
        pending.append(copy)
        return copy

    def block(j):
        return pl.ds(pl.multiple_of(j * cols, cols), cols)

    def part(buf, rows, j):
        return buf.at[rows, block(j)]

    def gather_start(buf, slot, pieces):
        near, far = [], []
        size = slots // pieces
        for p in range(pieces):
            rows = pl.ds(p * size, size)
            mine_part = part(buf, rows, f)
            far.append(to_feat(slot + 1, p, mine_part, mine_part, across))
            near.append(to_feat(slot, p, mine_part, mine_part, partner))
        return near, far

    def relay(buf, slot, pieces, p):
        size = slots // pieces
        got = part(buf, pl.ds(p * size, size), across)
        return to_feat(slot + 2, p, got, got, partner)

    def arrived(copies):
        for copy in copies:
            copy.wait_recv()

    loads[0].wait()
    inc = inc_ref[...]
    vrow = inc[0:1, :]
    meta[...] = jnp.zeros_like(meta)
    meta[0:1, :] = vrow.astype(jnp.float32)
    meta[1:2, :] = inc[1:2, :].astype(jnp.float32)
    meta[2:3, :] = inc[2:3, :].astype(jnp.float32)
    wrow = meta[2:3, :]
    columns = jnp.transpose(meta[...])
    vcol = columns[:, 0:1].astype(jnp.int32)
    wcol = columns[:, 2:3]
    same = vcol == vrow
    v_mask[...] = jnp.where(same, 1.0, 0.0).astype(jnp.bfloat16)
    dvis_row = lax.rsqrt(1.0 + jnp.sum(jnp.where(same, wcol, 0.0), axis=0, keepdims=True))
    meta[3:4, :] = wrow * dvis_row

    mine = lax.rem(d, 2)
    for o in range(owners):
        tile = meta[:, o // 2 * LANES : (o // 2 + 1) * LANES]
        moved = pltpu.roll(tile, cap, 1)
        meta_send[o] = jnp.where(mine == o % 2, tile, moved)

    pl.semaphore_wait(barrier, owners - 1 + feats - 1)
    meta_copies = to_owners(0, meta_send, meta_recv)

    loads[1].wait()
    loads[2].wait()
    picked = jnp.zeros((slots, 2 * cols), jnp.float32)
    step = 512
    lane = lax.broadcasted_iota(jnp.int32, (slots, step), 1)
    for base in range(0, nvert, step):
        hit = jnp.where(vcol - base == lane, 1.0, 0.0).astype(jnp.bfloat16)
        both = jnp.concatenate(
            [feat_ref[base : base + step, :], cot_ref[base : base + step, :]], axis=1
        )
        picked = picked + jnp.dot(hit, both, preferred_element_type=jnp.float32)
    x_send[...] = picked[:, :cols].astype(jnp.bfloat16).reshape(owners, cap, cols)
    x_copies = to_owners(1, x_send, x_recv)
    cot[:, block(f)] = picked[:, cols:].astype(jnp.bfloat16)

    loads[3].wait()
    theta[:, block(f)] = theta_ref[...]
    theta_near, theta_far = gather_start(theta, 0, feats)
    cot_near, cot_far = gather_start(cot, 3, feats)

    dvis = lax.rsqrt(1.0 + jnp.sum(jnp.where(same, wrow, 0.0), axis=1, keepdims=True))
    scale = wcol * dvis
    sub_i = lax.broadcasted_iota(jnp.int32, (slots, slots), 0)
    lane_i = lax.broadcasted_iota(jnp.int32, (slots, slots), 1)
    later_row = jnp.sum(
        jnp.where(same, jnp.where(sub_i < lane_i, 1.0, 0.0), 0.0), axis=0, keepdims=True
    )
    later_col = jnp.sum(
        jnp.where(same, jnp.where(lane_i < sub_i, 1.0, 0.0), 0.0), axis=1, keepdims=True
    )
    rep_ref[...] = jnp.where(later_row > 0.0, -1, vrow)

    arrived(meta_copies)
    half = lax.broadcasted_iota(jnp.int32, (8, LANES), 1) < cap
    for q in range(owners // 2):
        meta_edge[:, q * LANES : (q + 1) * LANES] = jnp.where(
            half, meta_recv[2 * q], meta_recv[2 * q + 1]
        )
    ecolumns = jnp.transpose(meta_edge[...])
    ecol = ecolumns[:, 1:2]
    same_edge = ecol == meta_edge[1:2, :]
    e_mask[...] = jnp.where(same_edge, 1.0, 0.0).astype(jnp.bfloat16)
    degree = 1.0 + jnp.sum(
        jnp.where(same_edge, meta_edge[2:3, :], 0.0), axis=1, keepdims=True
    )
    sent_scale = ecolumns[:, 3:4]
    eint = ecol.astype(jnp.int32)
    loads[4].wait()
    groups = ew_ref.shape[0]
    eweight = jnp.zeros((slots, LANES), jnp.float32)
    for g in range(groups):
        near = lax.broadcasted_iota(jnp.int32, (slots, LANES), 1) + g * LANES
        eweight = jnp.where(eint == near, ew_ref[g : g + 1, :], eweight)
    edge_scale = jnp.sum(eweight, axis=1, keepdims=True) / degree

    arrived(x_copies)
    rows = x_recv[...].reshape(slots, cols).astype(jnp.float32) * sent_scale
    b_send[...] = (
        (edge_scale * hi_lo_dot(e_mask[...], rows))
        .astype(jnp.bfloat16)
        .reshape(owners, cap, cols)
    )
    b_copies = to_owners(2, b_send, b_recv)

    theta_relay, cot_relay = [], []
    for p in range(feats):
        theta_far[p].wait_recv()
        theta_relay.append(relay(theta, 0, feats, p))
    for p in range(feats):
        cot_far[p].wait_recv()
        cot_relay.append(relay(cot, 3, feats, p))

    arrived(b_copies)
    back = wcol * b_recv[...].reshape(slots, cols).astype(jnp.float32)
    ax[:, block(f)] = (dvis * hi_lo_dot(v_mask[...], back)).astype(jnp.bfloat16)
    ax_near, ax_far = gather_start(ax, 6, feats)
    arrived(theta_near + theta_relay + cot_near + cot_relay)

    gx_copies = []
    size = slots // feats
    per_piece = size // cap

    def piece(p):
        rows = pl.ds(p * size, size)
        summed = jnp.dot(ax[rows, :], theta[...], preferred_element_type=jnp.float32)
        sigma = jax.nn.sigmoid(summed)
        slope = sigma * (1.0 + summed * (1.0 - sigma))
        grad = (cot[rows, :].astype(jnp.float32) * slope).astype(jnp.bfloat16)
        acts[rows, :] = (summed * sigma).astype(jnp.bfloat16)
        grads[rows, :] = grad
        turned = lax.dot_general(
            grad,
            theta[block(f), :],
            (((1,), (1,)), ((), ())),
            preferred_element_type=jnp.float32,
        )
        message = scale[p * size : (p + 1) * size] * turned
        gx_send[p * per_piece : (p + 1) * per_piece] = message.astype(jnp.bfloat16).reshape(
            per_piece, cap, cols
        )

    ax_relay = []
    for p in range(feats):
        ax_far[p].wait_recv()
        ax_relay.append(relay(ax, 6, feats, p))
        if p:
            ax_near[p - 1].wait_recv()
            ax_relay[p - 1].wait_recv()
            piece(p - 1)
    ax_near[feats - 1].wait_recv()
    ax_relay[feats - 1].wait_recv()
    piece(feats - 1)
    gx_copies = to_owners(3, gx_send, gx_recv)

    once = jnp.where(later_col > 0.0, 0.0, grads[:, block(f)].astype(jnp.float32))
    term[...] = lax.dot_general(
        ax[...],
        once.astype(jnp.bfloat16),
        (((0,), (0,)), ((), ())),
        preferred_element_type=jnp.float32,
    ).reshape(owners, share, cols)
    term_copies = to_owners(5, term, term_recv)
    act_ref[...] = acts[:, block(f)]

    arrived(gx_copies)
    esum = jnp.dot(
        e_mask[...], gx_recv[...].reshape(slots, cols), preferred_element_type=jnp.float32
    )
    gb_send[...] = (edge_scale * esum).astype(jnp.bfloat16).reshape(owners, cap, cols)
    gb_copies = to_owners(4, gb_send, gb_recv)

    arrived(gb_copies)
    gback = wcol * gb_recv[...].reshape(slots, cols).astype(jnp.float32)
    gf_ref[...] = (dvis * hi_lo_dot(v_mask[...], gback)).astype(jnp.bfloat16)
    arrived(term_copies)
    gt_ref[...] = jnp.sum(term_recv[...], axis=0)
    for copy in pending:
        copy.wait_send()


def spread_kernel(rep_ref, act_ref, gf_ref, gt_ref, act_out, gf_out, gt_out):
    rows, cols = act_out.shape
    slots = act_ref.shape[0]
    base = pl.program_id(0) * rows
    vertex = lax.broadcasted_iota(jnp.int32, (rows, slots), 0) + base
    hit = jnp.where(vertex == rep_ref[...], 1.0, 0.0).astype(jnp.bfloat16)
    both = jnp.concatenate([act_ref[...], gf_ref[...]], axis=1)
    out = jnp.dot(hit, both, preferred_element_type=jnp.float32)
    act_out[...] = out[:, :cols].astype(act_out.dtype)
    gf_out[...] = out[:, cols:].astype(gf_out.dtype)
    gt_out[...] = gt_ref[...]


def compact(features, theta, incidence, edge_weight, cotangent):
    owners = lax.axis_size("dom")
    feats = lax.axis_size("feat")
    nvert, cols = features.shape
    slots = incidence.shape[1]
    cap = slots // owners
    share = theta.shape[0] // owners
    whole_theta = (theta.shape[0], feats * cols)
    bf16, f32 = jnp.bfloat16, jnp.float32
    vmem = pl.BlockSpec(memory_space=pltpu.VMEM)
    block = pltpu.VMEM((owners, cap, cols), bf16)
    act, gf, gt, rep = pl.pallas_call(
        layer_kernel,
        out_shape=(
            jax.ShapeDtypeStruct((slots, cols), bf16),
            jax.ShapeDtypeStruct((slots, cols), bf16),
            jax.ShapeDtypeStruct((share, cols), f32),
            jax.ShapeDtypeStruct((1, slots), jnp.int32),
        ),
        in_specs=[pl.BlockSpec(memory_space=pltpu.HBM)] * 5,
        out_specs=(vmem,) * 4,
        scratch_shapes=[
            pltpu.VMEM(features.shape, bf16),
            pltpu.VMEM(theta.shape, bf16),
            pltpu.VMEM(incidence.shape, jnp.int32),
            pltpu.VMEM((edge_weight.shape[0] // LANES, LANES), f32),
            pltpu.VMEM(cotangent.shape, bf16),
            pltpu.SemaphoreType.DMA((5,)),
            pltpu.VMEM((8, slots), f32),
            pltpu.VMEM((owners, 8, LANES), f32),
            pltpu.VMEM((owners, 8, LANES), f32),
            pltpu.VMEM((8, slots), f32),
            pltpu.VMEM((slots, slots), bf16),
            pltpu.VMEM((slots, slots), bf16),
        ]
        + [block] * 8
        + [
            pltpu.VMEM(whole_theta, bf16),
            pltpu.VMEM((slots, feats * cols), bf16),
            pltpu.VMEM((slots, feats * cols), bf16),
            pltpu.VMEM((slots, feats * cols), bf16),
            pltpu.VMEM((slots, feats * cols), bf16),
            pltpu.VMEM((owners, share, cols), f32),
            pltpu.VMEM((owners, share, cols), f32),
            pltpu.SemaphoreType.DMA((6, owners - 1)),
            pltpu.SemaphoreType.DMA((6, owners - 1)),
            pltpu.SemaphoreType.DMA((9, feats)),
            pltpu.SemaphoreType.DMA((9, feats)),
        ],
        compiler_params=pltpu.CompilerParams(
            collective_id=0, has_side_effects=True, vmem_limit_bytes=VMEM_BYTES
        ),
        name="layer",
    )(features, theta, incidence, edge_weight.reshape(-1, LANES), cotangent)
    rows = 1024
    whole = lambda i: (0, 0)
    activation, grad_features, grad_theta = pl.pallas_call(
        spread_kernel,
        grid=(nvert // rows,),
        out_shape=(jax.ShapeDtypeStruct((nvert, cols), bf16),) * 2
        + (jax.ShapeDtypeStruct((share, cols), f32),),
        in_specs=[
            pl.BlockSpec((1, slots), whole),
            pl.BlockSpec((slots, cols), whole),
            pl.BlockSpec((slots, cols), whole),
            pl.BlockSpec((share, cols), whole),
        ],
        out_specs=(pl.BlockSpec((rows, cols), lambda i: (i, 0)),) * 2
        + (pl.BlockSpec((share, cols), whole),),
        compiler_params=pltpu.CompilerParams(vmem_limit_bytes=VMEM_BYTES),
        name="spread",
    )(rep, act, gf, gt)
    return activation, grad_features, grad_theta


def local(features, theta, incidence, edge_weight, cotangent):
    owners = lax.axis_size("dom")
    nvert = features.shape[0]
    cols = features.shape[1]
    nedge = edge_weight.shape[0]
    vert = incidence[0]
    edge = incidence[1]
    weight = incidence[2]
    weight_f = weight.astype(jnp.float32)
    dvis = lax.rsqrt(1.0 + jax.ops.segment_sum(weight_f, vert, num_segments=nvert))
    slot_scale = weight_f * dvis[vert]
    full_rows = lax.all_gather(features, "feat", axis=1, tiled=True)
    projected = jnp.dot(full_rows, theta, preferred_element_type=jnp.float32).astype(jnp.bfloat16)
    message = (slot_scale[:, None] * projected[vert].astype(jnp.float32)).astype(jnp.bfloat16)
    recv_rows, recv_edge, recv_weight = (
        lax.all_to_all(
            message.reshape(owners, -1, cols), "dom", split_axis=0, concat_axis=0, tiled=True
        ),
        lax.all_to_all(edge.reshape(owners, -1), "dom", split_axis=0, concat_axis=0, tiled=True),
        lax.all_to_all(weight.reshape(owners, -1), "dom", split_axis=0, concat_axis=0, tiled=True),
    )
    recv_edge = recv_edge.reshape(-1)
    degree = 1.0 + jax.ops.segment_sum(
        recv_weight.reshape(-1).astype(jnp.float32), recv_edge, num_segments=nedge
    )
    edge_scale = edge_weight / degree

    def edge_side(rows):
        edge_sum = jax.ops.segment_sum(
            rows.reshape(-1, cols).astype(jnp.float32), recv_edge, num_segments=nedge
        )
        edge_rows = (edge_scale[:, None] * edge_sum).astype(jnp.bfloat16)
        return edge_rows[recv_edge].reshape(owners, -1, cols)

    def vertex_side(back):
        terms = weight_f[:, None] * back.reshape(-1, cols).astype(jnp.float32)
        return dvis[:, None] * jax.ops.segment_sum(terms, vert, num_segments=nvert)

    back = lax.all_to_all(edge_side(recv_rows), "dom", split_axis=0, concat_axis=0, tiled=True)
    summed = vertex_side(back)
    sigma = jax.nn.sigmoid(summed)
    activation = (summed * sigma).astype(jnp.bfloat16)
    slope = sigma * (1.0 + summed * (1.0 - sigma))
    grad_summed = cotangent.astype(jnp.float32) * slope
    grad_message = (slot_scale[:, None] * grad_summed[vert]).astype(jnp.bfloat16)
    grad_recv = lax.all_to_all(
        grad_message.reshape(owners, -1, cols), "dom", split_axis=0, concat_axis=0, tiled=True
    )
    grad_back = lax.all_to_all(edge_side(grad_recv), "dom", split_axis=0, concat_axis=0, tiled=True)
    grad_projected = vertex_side(grad_back).astype(jnp.bfloat16)
    theta_full = lax.all_gather(theta, "feat", axis=1, tiled=True)
    theta_mine = lax.dynamic_slice_in_dim(theta_full, lax.axis_index("feat") * cols, cols, 0)
    grad_total = lax.dot_general(
        lax.all_gather(grad_projected, "feat", axis=1, tiled=True),
        theta_mine,
        (((1,), (1,)), ((), ())),
        preferred_element_type=jnp.float32,
    )
    grad_features = grad_total.astype(jnp.bfloat16)
    share = full_rows.shape[1] // owners
    term = lax.dot_general(
        full_rows, grad_projected, (((0,), (0,)), ((), ())), preferred_element_type=jnp.float32
    )
    total = lax.psum(term, "dom")
    grad_theta = lax.dynamic_slice_in_dim(total, lax.axis_index("dom") * share, share, 0)
    return (activation, grad_features, grad_theta)


def solution(mesh):
    placed = (P("dom", "feat"), P(None, "feat"), P(None, "dom"), P("dom"), P("dom", "feat"))
    owners, feats = mesh.shape["dom"], mesh.shape["feat"]

    def program(features, theta, incidence, edge_weight, cotangent):
        nvert, cols = features.shape
        slots, nedge = incidence.shape[1], edge_weight.shape[0]
        fits = (
            feats == 4
            and cols == LANES
            and owners % 2 == 0
            and slots == owners * LANES // 2
            and slots == theta.shape[0] == feats * cols
            and nvert % 1024 == 0
            and nedge % LANES == 0
            and theta.shape[0] % (16 * owners) == 0
            and cols % (theta.shape[0] // owners) == 0
        )
        run = compact if fits else local
        return run(features, theta, incidence, edge_weight, cotangent)

    return jax.shard_map(
        program,
        mesh=mesh,
        in_specs=placed,
        out_specs=(P("dom", "feat"), P("dom", "feat"), P("dom", "feat")),
        check_vma=False,
    )
```

```python
import functools

import jax
import jax.numpy as jnp
from jax import lax
from jax.experimental import pallas as pl
from jax.experimental.pallas import tpu as pltpu
from jax.sharding import PartitionSpec as P

MESH = pl.DeviceIdType.MESH
LANES = 128
VMEM_BYTES = 62 * 1024 * 1024


def hi_lo_dot(mask, rows):
    hi = rows.astype(jnp.bfloat16)
    lo = (rows - hi.astype(jnp.float32)).astype(jnp.bfloat16)
    both = jnp.concatenate([hi, lo], axis=1)
    out = jnp.dot(mask, both, preferred_element_type=jnp.float32)
    half = rows.shape[1]
    return out[:, :half] + out[:, half:]


def layer_kernel(
    feat_hbm, theta_hbm, inc_hbm, ew_hbm, cot_hbm,
    act_ref, gf_ref, gt_ref, rep_ref,
    feat_ref, theta_ref, inc_ref, ew_ref, cot_ref, load_sem,
    meta, meta_send, meta_recv, meta_edge, v_mask, e_mask,
    x_send, x_recv, b_send, b_recv, gx_send, gx_recv, gb_send, gb_recv,
    theta, cot, ax, grads, acts, term, term_recv,
    dom_send, dom_recv, feat_send, feat_recv,
):
    owners, cap, cols = x_send.shape
    slots = ax.shape[0]
    feats = ax.shape[1] // cols
    nvert = feat_ref.shape[0]
    share = gt_ref.shape[0]
    d = lax.axis_index("dom")
    f = lax.axis_index("feat")
    partner = f + 1 - 2 * lax.rem(f, 2)
    across = lax.rem(f + 2, 4)
    diagonal = lax.rem(partner + 2, 4)

    loads = []
    for n, (src, dst) in enumerate(
        (
            (inc_hbm, inc_ref),
            (feat_hbm, feat_ref),
            (cot_hbm, cot_ref),
            (theta_hbm, theta_ref),
            (ew_hbm, ew_ref),
        )
    ):
        load = pltpu.make_async_copy(src, dst, load_sem.at[n])
        load.start()
        loads.append(load)

    barrier = pltpu.get_barrier_semaphore()
    for k in range(1, owners):
        pl.semaphore_signal(
            barrier, inc=1, device_id=(lax.rem(d + k, owners), f), device_id_type=MESH
        )
    for other in (partner, across, diagonal):
        pl.semaphore_signal(barrier, inc=1, device_id=(d, other), device_id_type=MESH)

    pending = []

    def to_owners(phase, src, dst):
        copies = []
        for k in range(1, owners):
            peer = lax.rem(d + k, owners)
            copy = pltpu.make_async_remote_copy(
                src_ref=src.at[peer],
                dst_ref=dst.at[d],
                send_sem=dom_send.at[phase, k - 1],
                recv_sem=dom_recv.at[phase, k - 1],
                device_id=(peer, f),
                device_id_type=MESH,
            )
            copy.start()
            copies.append(copy)
        pending.extend(copies)
        dst[d] = src[d]
        return copies

    def to_feat(slot, p, src, dst, other):
        copy = pltpu.make_async_remote_copy(
            src_ref=src,
            dst_ref=dst,
            send_sem=feat_send.at[slot, p],
            recv_sem=feat_recv.at[slot, p],
            device_id=(d, other),
            device_id_type=MESH,
        )
        copy.start()
        pending.append(copy)
        return copy

    def block(j):
        return pl.ds(pl.multiple_of(j * cols, cols), cols)

    def part(buf, rows, j):
        return buf.at[rows, block(j)]

    def gather_start(buf, slot, pieces):
        near, far = [], []
        size = slots // pieces
        for p in range(pieces):
            rows = pl.ds(p * size, size)
            mine_part = part(buf, rows, f)
            far.append(to_feat(slot + 1, p, mine_part, mine_part, across))
            near.append(to_feat(slot, p, mine_part, mine_part, partner))
        return near, far

    def relay(buf, slot, pieces, p):
        size = slots // pieces
        got = part(buf, pl.ds(p * size, size), across)
        return to_feat(slot + 2, p, got, got, partner)

    def arrived(copies):
        for copy in copies:
            copy.wait_recv()

    loads[0].wait()
    inc = inc_ref[...]
    vrow = inc[0:1, :]
    meta[...] = jnp.zeros_like(meta)
    meta[0:1, :] = vrow.astype(jnp.float32)
    meta[1:2, :] = inc[1:2, :].astype(jnp.float32)
    meta[2:3, :] = inc[2:3, :].astype(jnp.float32)
    wrow = meta[2:3, :]
    columns = jnp.transpose(meta[...])
    vcol = columns[:, 0:1].astype(jnp.int32)
    wcol = columns[:, 2:3]
    same = vcol == vrow
    v_mask[...] = jnp.where(same, 1.0, 0.0).astype(jnp.bfloat16)
    dvis_row = lax.rsqrt(1.0 + jnp.sum(jnp.where(same, wcol, 0.0), axis=0, keepdims=True))
    meta[3:4, :] = wrow * dvis_row

    mine = lax.rem(d, 2)
    for o in range(owners):
        tile = meta[:, o // 2 * LANES : (o // 2 + 1) * LANES]
        moved = pltpu.roll(tile, cap, 1)
        meta_send[o] = jnp.where(mine == o % 2, tile, moved)

    pl.semaphore_wait(barrier, owners - 1 + feats - 1)
    meta_copies = to_owners(0, meta_send, meta_recv)

    loads[1].wait()
    loads[2].wait()
    picked = jnp.zeros((slots, 2 * cols), jnp.float32)
    step = 512
    lane = lax.broadcasted_iota(jnp.int32, (slots, step), 1)
    for base in range(0, nvert, step):
        hit = jnp.where(vcol - base == lane, 1.0, 0.0).astype(jnp.bfloat16)
        both = jnp.concatenate(
            [feat_ref[base : base + step, :], cot_ref[base : base + step, :]], axis=1
        )
        picked = picked + jnp.dot(hit, both, preferred_element_type=jnp.float32)
    x_send[...] = picked[:, :cols].astype(jnp.bfloat16).reshape(owners, cap, cols)
    x_copies = to_owners(1, x_send, x_recv)
    cot[:, block(f)] = picked[:, cols:].astype(jnp.bfloat16)

    loads[3].wait()
    theta[:, block(f)] = theta_ref[...]
    theta_near, theta_far = gather_start(theta, 0, feats)
    cot_near, cot_far = gather_start(cot, 3, feats)

    dvis = lax.rsqrt(1.0 + jnp.sum(jnp.where(same, wrow, 0.0), axis=1, keepdims=True))
    scale = wcol * dvis
    sub_i = lax.broadcasted_iota(jnp.int32, (slots, slots), 0)
    lane_i = lax.broadcasted_iota(jnp.int32, (slots, slots), 1)
    later_row = jnp.sum(
        jnp.where(same, jnp.where(sub_i < lane_i, 1.0, 0.0), 0.0), axis=0, keepdims=True
    )
    later_col = jnp.sum(
        jnp.where(same, jnp.where(lane_i < sub_i, 1.0, 0.0), 0.0), axis=1, keepdims=True
    )
    rep_ref[...] = jnp.where(later_row > 0.0, -1, vrow)

    arrived(meta_copies)
    half = lax.broadcasted_iota(jnp.int32, (8, LANES), 1) < cap
    for q in range(owners // 2):
        meta_edge[:, q * LANES : (q + 1) * LANES] = jnp.where(
            half, meta_recv[2 * q], meta_recv[2 * q + 1]
        )
    ecolumns = jnp.transpose(meta_edge[...])
    ecol = ecolumns[:, 1:2]
    same_edge = ecol == meta_edge[1:2, :]
    e_mask[...] = jnp.where(same_edge, 1.0, 0.0).astype(jnp.bfloat16)
    degree = 1.0 + jnp.sum(
        jnp.where(same_edge, meta_edge[2:3, :], 0.0), axis=1, keepdims=True
    )
    sent_scale = ecolumns[:, 3:4]
    eint = ecol.astype(jnp.int32)
    loads[4].wait()
    groups = ew_ref.shape[0]
    eweight = jnp.zeros((slots, LANES), jnp.float32)
    for g in range(groups):
        near = lax.broadcasted_iota(jnp.int32, (slots, LANES), 1) + g * LANES
        eweight = jnp.where(eint == near, ew_ref[g : g + 1, :], eweight)
    edge_scale = jnp.sum(eweight, axis=1, keepdims=True) / degree

    arrived(x_copies)
    rows = x_recv[...].reshape(slots, cols).astype(jnp.float32) * sent_scale
    b_send[...] = (
        (edge_scale * hi_lo_dot(e_mask[...], rows))
        .astype(jnp.bfloat16)
        .reshape(owners, cap, cols)
    )
    b_copies = to_owners(2, b_send, b_recv)

    theta_relay, cot_relay = [], []
    for p in range(feats):
        theta_far[p].wait_recv()
        theta_relay.append(relay(theta, 0, feats, p))
    for p in range(feats):
        cot_far[p].wait_recv()
        cot_relay.append(relay(cot, 3, feats, p))

    arrived(b_copies)
    back = wcol * b_recv[...].reshape(slots, cols).astype(jnp.float32)
    ax[:, block(f)] = (dvis * hi_lo_dot(v_mask[...], back)).astype(jnp.bfloat16)
    ax_near, ax_far = gather_start(ax, 6, feats)
    arrived(theta_near + theta_relay + cot_near + cot_relay)

    gx_copies = []
    size = slots // feats
    per_piece = size // cap

    def piece(p):
        rows = pl.ds(p * size, size)
        summed = jnp.dot(ax[rows, :], theta[...], preferred_element_type=jnp.float32)
        sigma = jax.nn.sigmoid(summed)
        slope = sigma * (1.0 + summed * (1.0 - sigma))
        grad = (cot[rows, :].astype(jnp.float32) * slope).astype(jnp.bfloat16)
        acts[rows, :] = (summed * sigma).astype(jnp.bfloat16)
        grads[rows, :] = grad
        turned = lax.dot_general(
            grad,
            theta[block(f), :],
            (((1,), (1,)), ((), ())),
            preferred_element_type=jnp.float32,
        )
        message = scale[p * size : (p + 1) * size] * turned
        gx_send[p * per_piece : (p + 1) * per_piece] = message.astype(jnp.bfloat16).reshape(
            per_piece, cap, cols
        )

    ax_relay = []
    for p in range(feats):
        ax_far[p].wait_recv()
        ax_relay.append(relay(ax, 6, feats, p))
        if p:
            ax_near[p - 1].wait_recv()
            ax_relay[p - 1].wait_recv()
            piece(p - 1)
    ax_near[feats - 1].wait_recv()
    ax_relay[feats - 1].wait_recv()
    piece(feats - 1)
    gx_copies = to_owners(3, gx_send, gx_recv)

    once = jnp.where(later_col > 0.0, 0.0, grads[:, block(f)].astype(jnp.float32))
    term[...] = lax.dot_general(
        ax[...],
        once.astype(jnp.bfloat16),
        (((0,), (0,)), ((), ())),
        preferred_element_type=jnp.float32,
    ).astype(jnp.bfloat16).reshape(owners, share, cols)
    act_ref[...] = acts[:, block(f)]

    arrived(gx_copies)
    esum = jnp.dot(
        e_mask[...], gx_recv[...].reshape(slots, cols), preferred_element_type=jnp.float32
    )
    gb_send[...] = (edge_scale * esum).astype(jnp.bfloat16).reshape(owners, cap, cols)
    gb_copies = to_owners(4, gb_send, gb_recv)
    term_copies = to_owners(5, term, term_recv)

    arrived(gb_copies)
    gback = wcol * gb_recv[...].reshape(slots, cols).astype(jnp.float32)
    gf_ref[...] = (dvis * hi_lo_dot(v_mask[...], gback)).astype(jnp.bfloat16)
    arrived(term_copies)
    gt_ref[...] = jnp.sum(term_recv[...].astype(jnp.float32), axis=0)
    for copy in pending:
        copy.wait_send()


def spread_kernel(rep_ref, act_ref, gf_ref, gt_ref, act_out, gf_out, gt_out):
    rows, cols = act_out.shape
    slots = act_ref.shape[0]
    base = pl.program_id(0) * rows
    vertex = lax.broadcasted_iota(jnp.int32, (rows, slots), 0) + base
    hit = jnp.where(vertex == rep_ref[...], 1.0, 0.0).astype(jnp.bfloat16)
    both = jnp.concatenate([act_ref[...], gf_ref[...]], axis=1)
    out = jnp.dot(hit, both, preferred_element_type=jnp.float32)
    act_out[...] = out[:, :cols].astype(act_out.dtype)
    gf_out[...] = out[:, cols:].astype(gf_out.dtype)
    gt_out[...] = gt_ref[...]


def compact(features, theta, incidence, edge_weight, cotangent):
    owners = lax.axis_size("dom")
    feats = lax.axis_size("feat")
    nvert, cols = features.shape
    slots = incidence.shape[1]
    cap = slots // owners
    share = theta.shape[0] // owners
    whole_theta = (theta.shape[0], feats * cols)
    bf16, f32 = jnp.bfloat16, jnp.float32
    vmem = pl.BlockSpec(memory_space=pltpu.VMEM)
    block = pltpu.VMEM((owners, cap, cols), bf16)
    act, gf, gt, rep = pl.pallas_call(
        layer_kernel,
        out_shape=(
            jax.ShapeDtypeStruct((slots, cols), bf16),
            jax.ShapeDtypeStruct((slots, cols), bf16),
            jax.ShapeDtypeStruct((share, cols), f32),
            jax.ShapeDtypeStruct((1, slots), jnp.int32),
        ),
        in_specs=[pl.BlockSpec(memory_space=pltpu.HBM)] * 5,
        out_specs=(vmem,) * 4,
        scratch_shapes=[
            pltpu.VMEM(features.shape, bf16),
            pltpu.VMEM(theta.shape, bf16),
            pltpu.VMEM(incidence.shape, jnp.int32),
            pltpu.VMEM((edge_weight.shape[0] // LANES, LANES), f32),
            pltpu.VMEM(cotangent.shape, bf16),
            pltpu.SemaphoreType.DMA((5,)),
            pltpu.VMEM((8, slots), f32),
            pltpu.VMEM((owners, 8, LANES), f32),
            pltpu.VMEM((owners, 8, LANES), f32),
            pltpu.VMEM((8, slots), f32),
            pltpu.VMEM((slots, slots), bf16),
            pltpu.VMEM((slots, slots), bf16),
        ]
        + [block] * 8
        + [
            pltpu.VMEM(whole_theta, bf16),
            pltpu.VMEM((slots, feats * cols), bf16),
            pltpu.VMEM((slots, feats * cols), bf16),
            pltpu.VMEM((slots, feats * cols), bf16),
            pltpu.VMEM((slots, feats * cols), bf16),
            pltpu.VMEM((owners, share, cols), bf16),
            pltpu.VMEM((owners, share, cols), bf16),
            pltpu.SemaphoreType.DMA((6, owners - 1)),
            pltpu.SemaphoreType.DMA((6, owners - 1)),
            pltpu.SemaphoreType.DMA((9, feats)),
            pltpu.SemaphoreType.DMA((9, feats)),
        ],
        compiler_params=pltpu.CompilerParams(
            collective_id=0, has_side_effects=True, vmem_limit_bytes=VMEM_BYTES
        ),
        name="layer",
    )(features, theta, incidence, edge_weight.reshape(-1, LANES), cotangent)
    rows = 2048
    whole = lambda i: (0, 0)
    activation, grad_features, grad_theta = pl.pallas_call(
        spread_kernel,
        grid=(nvert // rows,),
        out_shape=(jax.ShapeDtypeStruct((nvert, cols), bf16),) * 2
        + (jax.ShapeDtypeStruct((share, cols), f32),),
        in_specs=[
            pl.BlockSpec((1, slots), whole),
            pl.BlockSpec((slots, cols), whole),
            pl.BlockSpec((slots, cols), whole),
            pl.BlockSpec((share, cols), whole),
        ],
        out_specs=(pl.BlockSpec((rows, cols), lambda i: (i, 0)),) * 2
        + (pl.BlockSpec((share, cols), whole),),
        compiler_params=pltpu.CompilerParams(vmem_limit_bytes=VMEM_BYTES),
        name="spread",
    )(rep, act, gf, gt)
    return activation, grad_features, grad_theta


def local(features, theta, incidence, edge_weight, cotangent):
    owners = lax.axis_size("dom")
    nvert = features.shape[0]
    cols = features.shape[1]
    nedge = edge_weight.shape[0]
    vert = incidence[0]
    edge = incidence[1]
    weight = incidence[2]
    weight_f = weight.astype(jnp.float32)
    dvis = lax.rsqrt(1.0 + jax.ops.segment_sum(weight_f, vert, num_segments=nvert))
    slot_scale = weight_f * dvis[vert]
    full_rows = lax.all_gather(features, "feat", axis=1, tiled=True)
    projected = jnp.dot(full_rows, theta, preferred_element_type=jnp.float32).astype(jnp.bfloat16)
    message = (slot_scale[:, None] * projected[vert].astype(jnp.float32)).astype(jnp.bfloat16)
    recv_rows, recv_edge, recv_weight = (
        lax.all_to_all(
            message.reshape(owners, -1, cols), "dom", split_axis=0, concat_axis=0, tiled=True
        ),
        lax.all_to_all(edge.reshape(owners, -1), "dom", split_axis=0, concat_axis=0, tiled=True),
        lax.all_to_all(weight.reshape(owners, -1), "dom", split_axis=0, concat_axis=0, tiled=True),
    )
    recv_edge = recv_edge.reshape(-1)
    degree = 1.0 + jax.ops.segment_sum(
        recv_weight.reshape(-1).astype(jnp.float32), recv_edge, num_segments=nedge
    )
    edge_scale = edge_weight / degree

    def edge_side(rows):
        edge_sum = jax.ops.segment_sum(
            rows.reshape(-1, cols).astype(jnp.float32), recv_edge, num_segments=nedge
        )
        edge_rows = (edge_scale[:, None] * edge_sum).astype(jnp.bfloat16)
        return edge_rows[recv_edge].reshape(owners, -1, cols)

    def vertex_side(back):
        terms = weight_f[:, None] * back.reshape(-1, cols).astype(jnp.float32)
        return dvis[:, None] * jax.ops.segment_sum(terms, vert, num_segments=nvert)

    back = lax.all_to_all(edge_side(recv_rows), "dom", split_axis=0, concat_axis=0, tiled=True)
    summed = vertex_side(back)
    sigma = jax.nn.sigmoid(summed)
    activation = (summed * sigma).astype(jnp.bfloat16)
    slope = sigma * (1.0 + summed * (1.0 - sigma))
    grad_summed = cotangent.astype(jnp.float32) * slope
    grad_message = (slot_scale[:, None] * grad_summed[vert]).astype(jnp.bfloat16)
    grad_recv = lax.all_to_all(
        grad_message.reshape(owners, -1, cols), "dom", split_axis=0, concat_axis=0, tiled=True
    )
    grad_back = lax.all_to_all(edge_side(grad_recv), "dom", split_axis=0, concat_axis=0, tiled=True)
    grad_projected = vertex_side(grad_back).astype(jnp.bfloat16)
    theta_full = lax.all_gather(theta, "feat", axis=1, tiled=True)
    theta_mine = lax.dynamic_slice_in_dim(theta_full, lax.axis_index("feat") * cols, cols, 0)
    grad_total = lax.dot_general(
        lax.all_gather(grad_projected, "feat", axis=1, tiled=True),
        theta_mine,
        (((1,), (1,)), ((), ())),
        preferred_element_type=jnp.float32,
    )
    grad_features = grad_total.astype(jnp.bfloat16)
    share = full_rows.shape[1] // owners
    term = lax.dot_general(
        full_rows, grad_projected, (((0,), (0,)), ((), ())), preferred_element_type=jnp.float32
    )
    total = lax.psum(term, "dom")
    grad_theta = lax.dynamic_slice_in_dim(total, lax.axis_index("dom") * share, share, 0)
    return (activation, grad_features, grad_theta)


def solution(mesh):
    placed = (P("dom", "feat"), P(None, "feat"), P(None, "dom"), P("dom"), P("dom", "feat"))
    owners, feats = mesh.shape["dom"], mesh.shape["feat"]

    def program(features, theta, incidence, edge_weight, cotangent):
        nvert, cols = features.shape
        slots, nedge = incidence.shape[1], edge_weight.shape[0]
        fits = (
            feats == 4
            and cols == LANES
            and owners % 2 == 0
            and slots == owners * LANES // 2
            and slots == theta.shape[0] == feats * cols
            and nvert % 1024 == 0
            and nedge % LANES == 0
            and theta.shape[0] % (16 * owners) == 0
            and cols % (theta.shape[0] // owners) == 0
        )
        run = compact if fits else local
        return run(features, theta, incidence, edge_weight, cotangent)

    return jax.shard_map(
        program,
        mesh=mesh,
        in_specs=placed,
        out_specs=(P("dom", "feat"), P("dom", "feat"), P("dom", "feat")),
        check_vma=False,
    )
```
